32 devices in a mesh: row: 4 (over z), col: 8 (over y, x, core).
Axes of the slice: x: 2, y: 2, z: 4, core: 2. Of those that a mesh axis runs over, the one named last changes fastest.
Arguments:
- tokens: bfloat16 [576, 8192], P('col', 'row'), may hold values from -6 to 6
- out_grad: bfloat16 [576, 8192], P('col', 'row'), may hold values from -6 to 6
- gate_pre: bfloat16 [576, 28672], P('row', 'col'), may hold values from -8 to 8
- up_pre: bfloat16 [576, 28672], P('row', 'col'), may hold values from -6 to 6
- w_gate: bfloat16 [8192, 28672], P('row', 'col'), may hold values from -0.125 to 0.125
- w_up: bfloat16 [8192, 28672], P('row', 'col'), may hold values from -0.125 to 0.125
- w_down: bfloat16 [28672, 8192], P('col', 'row'), may hold values from -0.0625 to 0.0625
- mask_gate: int32 [128, 448], P('row', 'col'), may hold values 0 or 1
- mask_up: int32 [128, 448], P('row', 'col'), may hold values 0 or 1
- mask_down: int32 [448, 128], P('col', 'row'), may hold values 0 or 1
Outputs:
- grad_x: bfloat16 [576, 8192], P('col', 'row')
- grad_gate: bfloat16 [8192, 28672], P('row', 'col')
- grad_up: bfloat16 [8192, 28672], P('row', 'col')
- grad_down: bfloat16 [28672, 8192], P('col', 'row')
The draws below stay inside these ranges and needn't reach their ends.
All inputs are finite; a program needn't handle non-finite values. No bound on the sum of `mask_gate` or of `mask_up` or of `mask_down` on one device may be relied on, other than what follows from the above.
Results may differ from the reference program's by a relative error of at most 0.0049.
Values may be sent and summed in bfloat16 or wider, within the bound.
No kernel may reach another device: no remote copies, remote signals or barrier semaphores. Data moves between devices by JAX's collectives and lax.ppermute only.
A program may use at most 192 MiB of HBM per device.

```python
import jax
import jax.numpy as jnp
from jax import lax

D = 8192
FF = 28672
TILE = 64
TOKENS = 576


def with_ends(drawn, own_key, smallest, high):
    longest = drawn.shape.index(max(drawn.shape))
    spots = []
    for shift in (0, 1):
        where = [jax.random.randint(jax.random.fold_in(own_key, axis), (), 0, length) for axis, length in enumerate(drawn.shape)]
        where[longest] = (where[longest] + shift) % drawn.shape[longest]
        spots.append(tuple(where))
    return drawn.at[spots[0]].set(smallest).at[spots[1]].set(high)


def steps_of(key, shape, cuts, least, top_value):
    loudness, own = 1.0, jax.random.fold_in(key, 6)
    for dim, blocks in cuts:
        steps = jnp.exp(jax.random.uniform(jax.random.fold_in(own, dim), (blocks,), jnp.float32, least / len(cuts), top_value / len(cuts)))
        loudness = loudness * jnp.repeat(steps, shape[dim] // blocks).reshape([-1 if axis == dim else 1 for axis in range(len(shape))])
    return loudness


def normal_values(key, shape, deviation, bound, split=(), dtype=jnp.bfloat16):
    entries = deviation * jax.random.normal(key, shape, jnp.float32)
    if split:
        entries = entries * steps_of(key, shape, split, -0.22, 0.18)
    return jnp.clip(entries, -bound, bound).astype(dtype)


def setup_inputs(seed: int = 0) -> dict:
    splits = jax.random.split(jax.random.key(seed), 11)
    tokens = normal_values(splits[0], (TOKENS, D), 1.0, 6.0, ((0, 8), (1, 4)))
    out_grad = normal_values(splits[1], (TOKENS, D), 1.0, 6.0, ((0, 8), (1, 4)))
    gate_pre = normal_values(splits[2], (TOKENS, FF), 1.5, 8.0, ((0, 4), (1, 8)))
    up_pre = normal_values(splits[3], (TOKENS, FF), 1.0, 6.0, ((0, 4), (1, 8)))
    w_gate = normal_values(splits[4], (D, FF), (3 * D // 10) ** -0.5, 0.125, ((0, 4), (1, 8)))
    w_up = normal_values(splits[5], (D, FF), (3 * D // 10) ** -0.5, 0.125, ((0, 4), (1, 8)))
    w_down = normal_values(splits[6], (FF, D), (3 * FF // 10) ** -0.5, 0.0625, ((0, 8), (1, 4)))
    mask_gate = with_ends((jax.random.randint(splits[7], (D // TILE, FF // TILE), 0, 10) < 3).astype(jnp.int32), jax.random.fold_in(splits[7], 1), 0, 1)
    mask_up = with_ends((jax.random.randint(splits[8], (D // TILE, FF // TILE), 0, 10) < 3).astype(jnp.int32), jax.random.fold_in(splits[8], 1), 0, 1)
    mask_down = with_ends((jax.random.randint(splits[9], (FF // TILE, D // TILE), 0, 10) < 3).astype(jnp.int32), jax.random.fold_in(splits[9], 1), 0, 1)
    return dict(tokens=tokens, out_grad=out_grad, gate_pre=gate_pre, up_pre=up_pre, w_gate=w_gate, w_up=w_up, w_down=w_down, mask_gate=mask_gate, mask_up=mask_up, mask_down=mask_down)


def expand(keep_mask):
    small = keep_mask.astype(jnp.bfloat16)
    return jnp.repeat(jnp.repeat(small, TILE, axis=0), TILE, axis=1)


def contract_last(left, right):
    return lax.dot_general(left, right, (((1,), (1,)), ((), ())), preferred_element_type=jnp.float32)


def contract_first(left, right):
    return lax.dot_general(left, right, (((0,), (0,)), ((), ())), preferred_element_type=jnp.float32)


def reference(tokens, out_grad, gate_pre, up_pre, w_gate, w_up, w_down, mask_gate, mask_up, mask_down):
    keep_gate = expand(mask_gate)
    keep_up = expand(mask_up)
    keep_down = expand(mask_down)
    gate_eff = w_gate * keep_gate
    up_eff = w_up * keep_up
    down_eff = w_down * keep_down
    gate_val = gate_pre.astype(jnp.float32)
    up_val = up_pre.astype(jnp.float32)
    sigmoid_g = jax.nn.sigmoid(gate_val)
    silu_g = gate_val * sigmoid_g
    hidden = (silu_g * up_val).astype(jnp.bfloat16)
    d_hidden = contract_last(out_grad, down_eff)
    d_gate = (d_hidden * up_val * sigmoid_g * (1.0 + gate_val * (1.0 - sigmoid_g))).astype(jnp.bfloat16)
    d_up = (d_hidden * silu_g).astype(jnp.bfloat16)
    grad_x = (contract_last(d_gate, gate_eff) + contract_last(d_up, up_eff)).astype(jnp.bfloat16)
    grad_gate = (contract_first(tokens, d_gate) * keep_gate.astype(jnp.float32)).astype(jnp.bfloat16)
    grad_up = (contract_first(tokens, d_up) * keep_up.astype(jnp.float32)).astype(jnp.bfloat16)
    grad_down = (contract_first(hidden, out_grad) * keep_down.astype(jnp.float32)).astype(jnp.bfloat16)
    return grad_x, grad_gate, grad_up, grad_down
```

```python
import functools

import jax
import jax.numpy as jnp
from jax import lax
from jax.experimental import pallas as pl
from jax.experimental.pallas import tpu as pltpu
from jax.sharding import PartitionSpec as P

TILE = 64
VMEM_LIMIT = 56 * 1024 * 1024
BF16, F32 = jnp.bfloat16, jnp.float32


def params(n_axes=1):
    return pltpu.CompilerParams(
        dimension_semantics=("arbitrary",) * n_axes, vmem_limit_bytes=VMEM_LIMIT
    )


def whole(shape):
    return pl.BlockSpec(shape, lambda j, *_: (0,) * len(shape))


def masked(block, keep):
    rows = [
        block[r * TILE : (r + 1) * TILE] * keep[r : r + 1] for r in range(keep.shape[0])
    ]
    return jnp.concatenate(rows, axis=0)


def dhidden_kernel(n_low, grad_ref, w_ref, keep_ref, low_ref, high_ref):
    w_eff = masked(w_ref[...], keep_ref[0].astype(BF16))
    out = lax.dot_general(
        grad_ref[...], w_eff, (((1,), (1,)), ((), ())), preferred_element_type=F32
    )

    @pl.when(pl.program_id(0) < n_low)
    def _():
        low_ref[...] = out

    @pl.when(pl.program_id(0) >= n_low)
    def _():
        high_ref[...] = out


def dhidden_part(grad_all, w_down, keep_down, cut, ft):
    T, D = grad_all.shape
    F = w_down.shape[0]
    return pl.pallas_call(
        functools.partial(dhidden_kernel, cut // ft),
        out_shape=(
            jax.ShapeDtypeStruct((T, cut), F32),
            jax.ShapeDtypeStruct((T, F - cut), F32),
        ),
        grid=(F // ft,),
        in_specs=[
            whole((T, D)),
            pl.BlockSpec((ft, D), lambda j: (j, 0)),
            pl.BlockSpec((1, ft // TILE, D), lambda j: (j, 0, 0)),
        ],
        out_specs=[
            pl.BlockSpec((T, ft), lambda j: (0, jnp.minimum(j, cut // ft - 1))),
            pl.BlockSpec((T, ft), lambda j: (0, jnp.maximum(j - cut // ft, 0))),
        ],
        compiler_params=params(),
        cost_estimate=pl.CostEstimate(
            flops=2 * T * D * F, bytes_accessed=2 * D * F + 4 * T * F, transcendentals=0
        ),
        name="dhidden",
    )(grad_all, w_down, keep_down)


def in_order(at_ref, buf, pieces, rows, half=0):
    for s, piece in enumerate(pieces):
        start = pl.multiple_of(at_ref[s] * rows, 16)
        buf[pl.ds(start, rows), :] = piece[half * rows : (half + 1) * rows, :]
    return buf[: buf.shape[0] - rows, :]


def gate_parts(gate, up):
    gate_val, up_val = gate.astype(F32), up.astype(F32)
    sig = jax.nn.sigmoid(gate_val)
    return gate_val, up_val, sig, gate_val * sig


def down_kernel(n, rows, at_ref, *refs):
    pairs, refs = refs[:n], refs[n:]
    grad_ref, keep_ref = refs[:2]
    gdown_ref, buf = refs[-2:]
    gate = in_order(at_ref, buf, pairs, rows, 0)
    up = in_order(at_ref, buf, pairs, rows, 1)
    _, up_val, _, silu = gate_parts(gate, up)
    hidden = (silu * up_val).astype(BF16)
    out = lax.dot_general(
        hidden, grad_ref[...], (((0,), (0,)), ((), ())), preferred_element_type=F32
    )
    gdown_ref[...] = masked(out, keep_ref[0]).astype(BF16)


def down_grad(where, pairs, grad_all, keep_down, held, at, f, n_row, ft):
    T, D = grad_all.shape
    F = keep_down.shape[0] * ft
    rows, n = pairs[0].shape[0], len(pairs)
    first = held is None
    args = [where, *pairs, grad_all, keep_down]
    here = at // ft
    return pl.pallas_call(
        functools.partial(down_kernel, n, rows // 2),
        out_shape=jax.ShapeDtypeStruct((F, D), BF16),
        grid_spec=pltpu.PrefetchScalarGridSpec(
            num_scalar_prefetch=1,
            grid=(f // ft,),
            in_specs=[pl.BlockSpec((rows, ft), lambda j, *_: (0, j))] * n
            + [whole((T, D)), pl.BlockSpec((1, ft // TILE, D), lambda j, *_: (j + here, 0, 0))]
            + ([] if first else [pl.BlockSpec(memory_space=pl.ANY)]),
            out_specs=pl.BlockSpec((ft, D), lambda j, *_: (j + here, 0)),
            scratch_shapes=[pltpu.VMEM(((n_row + 1) * rows // 2, ft), BF16)],
        ),
        input_output_aliases={} if first else {len(args): 0},
        compiler_params=params(),
        cost_estimate=pl.CostEstimate(
            flops=2 * T * D * f, bytes_accessed=2 * D * f + 14 * T * f, transcendentals=T * f
        ),
        name="grad_down",
    )(*args, *([] if first else [held]))


def input_kernel(n, rows, first, at_ref, *refs):
    pieces, pairs, rest = refs[:n], refs[n : 2 * n], refs[2 * n :]
    wg_ref, wu_ref, kg_ref, ku_ref = rest[:4]
    rest = rest[4:]
    if not first:
        sum_ref, rest = rest[0], rest[1:]
    gx_ref, dg_ref, du_ref, buf = rest

    @pl.when(pl.program_id(0) == 0)
    def _():
        d_hidden = in_order(at_ref, buf, pieces, rows).astype(F32)
        gate = in_order(at_ref, buf, pairs, rows, 0)
        up = in_order(at_ref, buf, pairs, rows, 1)
        gate_val, up_val, sig, silu = gate_parts(gate, up)
        dg_ref[...] = (d_hidden * up_val * sig * (1.0 + gate_val * (1.0 - sig))).astype(BF16)
        du_ref[...] = (d_hidden * silu).astype(BF16)

    dims = (((1,), (1,)), ((), ()))
    wg = masked(wg_ref[...], kg_ref[...].astype(BF16))
    wu = masked(wu_ref[...], ku_ref[...].astype(BF16))
    out = lax.dot_general(dg_ref[...], wg, dims, preferred_element_type=F32)
    out = out + lax.dot_general(du_ref[...], wu, dims, preferred_element_type=F32)
    gx_ref[...] = out if first else sum_ref[...] + out


def input_grad(where, pieces, pairs, w_gate, w_up, keep_gate, keep_up, total, start, at, f, n_row, dt):
    rows = pieces[0].shape[0]
    T = rows * n_row
    D = w_gate.shape[0]
    n = len(pieces)
    col, inner = (start + at) // f, at // f
    first = total is None
    weight = pl.BlockSpec((dt, f), lambda d, *_: (d, col))
    keep = pl.BlockSpec((dt // TILE, f), lambda d, *_: (d, col))
    gx = pl.BlockSpec((T, dt), lambda d, *_: (0, d))
    args = [where, *pieces, *pairs, w_gate, w_up, keep_gate, keep_up]
    return pl.pallas_call(
        functools.partial(input_kernel, n, rows, first),
        out_shape=(
            jax.ShapeDtypeStruct((T, D), F32),
            jax.ShapeDtypeStruct((T, f), BF16),
            jax.ShapeDtypeStruct((T, f), BF16),
        ),
        grid_spec=pltpu.PrefetchScalarGridSpec(
            num_scalar_prefetch=1,
            grid=(D // dt,),
            in_specs=[pl.BlockSpec((rows, f), lambda d, *_: (0, inner))] * n
            + [pl.BlockSpec((2 * rows, f), lambda d, *_: (0, inner))] * n
            + [weight, weight, keep, keep]
            + ([] if first else [gx]),
            out_specs=[gx, whole((T, f)), whole((T, f))],
            scratch_shapes=[pltpu.VMEM(((n_row + 1) * rows, f), BF16)],
        ),
        input_output_aliases={} if first else {len(args): 0},
        compiler_params=params(),
        cost_estimate=pl.CostEstimate(
            flops=4 * T * D * f, bytes_accessed=4 * D * f + 8 * T * D, transcendentals=T * f
        ),
        name="grad_x_part",
    )(*args, *([] if first else [total]))


def weight_kernel(first, tok_ref, dg_ref, du_ref, kg_ref, ku_ref, *refs):
    gg_ref, gu_ref = refs[-2:]
    tok = tok_ref[...]
    dims = (((0,), (0,)), ((), ()))
    gg = lax.dot_general(tok, dg_ref[...], dims, preferred_element_type=F32)
    gg_ref[...] = masked(gg, kg_ref[...]).astype(BF16)
    gu = lax.dot_general(tok, du_ref[...], dims, preferred_element_type=F32)
    gu_ref[...] = masked(gu, ku_ref[...]).astype(BF16)


def weight_grads(tok_all, d_gate, d_up, keep_gate, keep_up, held, at, f, dt):
    T, D = tok_all.shape
    F = keep_gate.shape[1]
    col = at // f
    first = held is None
    keep = pl.BlockSpec((dt // TILE, f), lambda d: (d, col))
    out = pl.BlockSpec((dt, f), lambda d: (d, col))
    return pl.pallas_call(
        functools.partial(weight_kernel, first),
        out_shape=(jax.ShapeDtypeStruct((D, F), BF16),) * 2,
        grid=(D // dt,),
        in_specs=[pl.BlockSpec((T, dt), lambda d: (0, d)), whole((T, f)), whole((T, f)), keep, keep]
        + ([] if first else [pl.BlockSpec(memory_space=pl.ANY)] * 2),
        out_specs=[out, out],
        input_output_aliases={} if first else {5: 0, 6: 1},
        compiler_params=params(),
        cost_estimate=pl.CostEstimate(
            flops=4 * T * D * f, bytes_accessed=4 * D * f + 2 * T * D, transcendentals=0
        ),
        name="grad_gate_up",
    )(tok_all, d_gate, d_up, keep_gate, keep_up, *([] if first else held))


class Queue:
    def __init__(self, perm):
        self.perm, self.flying = perm, [(), ()]

    def hold(self, *deps):
        self.flying[0] = (*self.flying[0], *deps)

    def issue(self, x):
        wait = self.flying.pop(0)
        if wait:
            x, *_ = lax.optimization_barrier((x, *wait))
        x = lax.ppermute(x, "row", self.perm)
        self.flying.append((x,))
        return x


class Four:
    def __init__(self, me):
        self.me = me
        self.outer = Queue([(0, 1), (1, 0), (2, 3), (3, 2)])
        self.inner = Queue([(1, 2), (2, 1), (0, 0), (3, 3)])
        self.mid = (me == 1) | (me == 2)
        self.side = me // 2
        near, far = jnp.where(self.side == 0, 2, 1), jnp.where(self.side == 0, 3, 0)
        self.where = jnp.stack(
            [
                me,
                me ^ 1,
                jnp.where(self.mid, near, 4),
                jnp.where(self.mid, far, 4),
                jnp.where(self.mid, 4, near),
                jnp.where(self.mid, 4, far),
            ]
        ).astype(jnp.int32)


class Gather:
    def __init__(self, four, piece):
        self.four, self.own = four, piece

    def swap(self):
        self.next = self.four.outer.issue(self.own)

    def cross(self):
        self.near = self.four.inner.issue(self.own)

    def cross_next(self):
        self.far = self.four.inner.issue(self.next)

    def spread(self, outwards=None):
        send = self.near if outwards is None else jnp.where(self.four.mid, self.near, outwards)
        self.near_out = self.four.outer.issue(send)

    def spread_next(self):
        self.far_out = self.four.outer.issue(self.far)

    def pieces(self):
        return [self.own, self.next, self.near, self.far, self.near_out, self.far_out]


class Reduce:
    def __init__(self, four, part):
        self.four, self.part = four, part
        self.rows = part.shape[0] // 4

    def block(self, b, count=1):
        return lax.dynamic_slice_in_dim(self.part, b * self.rows, count * self.rows, 0)

    def others(self):
        return self.block(2 - 2 * self.four.side, 2)

    def cross(self, from_end):
        send = (self.others() + from_end.astype(F32)).astype(BF16)
        self.crossed = self.four.inner.issue(send)

    def crossed_block(self, b):
        got = lax.dynamic_slice_in_dim(self.crossed, (b % 2) * self.rows, self.rows, 0)
        return jnp.where(self.four.mid, got.astype(F32), 0.0)

    def swap(self):
        other = self.four.me ^ 1
        self.swapped = self.four.outer.issue(
            (self.block(other) + self.crossed_block(other)).astype(BF16)
        )

    def result(self):
        me = self.four.me
        return (self.block(me) + self.crossed_block(me) + self.swapped.astype(F32)).astype(BF16)


def ring_gather(piece, n):
    ring = [(i, (i + 1) % n) for i in range(n)]
    pieces = [piece]
    for _ in range(1, n):
        pieces.append(lax.ppermute(pieces[-1], "row", ring))
    return pieces


def ring_reduce(part, n, me):
    ring = [(i, (i + 1) % n) for i in range(n)]
    rows = part.shape[0] // n
    total = None
    for s in range(n):
        block = lax.dynamic_slice_in_dim(part, (me + n - 1 - s) % n * rows, rows, 0)
        total = block if total is None else block + total.astype(F32)
        total = total.astype(BF16)
        if s < n - 1:
            total = lax.ppermute(total, "row", ring)
    return total


def pairs_gather(piece, n, in_turn=False):
    got = [piece]
    for k in range(1, n // 2):
        send = lax.optimization_barrier((piece, got[-1]))[0] if in_turn else piece
        got.append(lax.ppermute(send, "col", [(i, i ^ (2 * k)) for i in range(n)]))
    return jnp.stack(got)


def pair_gather(mine, n, me):
    half, rows, width = mine.shape
    core, pair = me % 2, me // 2
    other = lax.ppermute(mine, "col", [(i, i ^ 1) for i in range(n)])
    even, odd = jnp.where(core == 0, mine, other), jnp.where(core == 0, other, mine)
    both = jnp.stack([even, odd], axis=1)
    ordered = [lax.dynamic_index_in_dim(both, pair ^ k, 0, keepdims=False) for k in range(half)]
    return jnp.stack(ordered).reshape(n * rows, width)


def pair_sums(part, n, me):
    rows = part.shape[0] // n
    core = me % 2
    blocks = part.reshape(n // 2, 2, rows, part.shape[1])
    send = lax.dynamic_index_in_dim(blocks, 1 - core, 1, keepdims=False)
    keep = lax.dynamic_index_in_dim(blocks, core, 1, keepdims=False)
    return keep + lax.ppermute(send, "col", [(i, i ^ 1) for i in range(n)])


def pair_reduce(summed, n, me):
    half = n // 2
    pair = me // 2
    total = lax.dynamic_index_in_dim(summed, pair, 0, keepdims=False)
    low = summed.astype(BF16)
    got = [
        lax.ppermute(
            lax.dynamic_index_in_dim(low, pair ^ k, 0, keepdims=False),
            "col",
            [(i, i ^ (2 * k)) for i in range(n)],
        )
        for k in range(1, half)
    ]
    for g in got:
        total = total + g.astype(F32)
    return total


def lanes(mask):
    return jnp.repeat(mask.astype(F32), TILE, axis=1)


def per_device(
    n_row,
    n_col,
    tokens,
    out_grad,
    gate_pre,
    up_pre,
    w_gate,
    w_up,
    w_down,
    mask_gate,
    mask_up,
    mask_down,
):
    row, col = lax.axis_index("row"), lax.axis_index("col")
    F, D = w_down.shape
    ft = 512 if F % 512 == 0 else 256
    dt = min(512, D)
    keep_gate, keep_up, keep_down = lanes(mask_gate), lanes(mask_up), lanes(mask_down)
    keep_down = keep_down.reshape(F // ft, ft // TILE, D)

    n_tiles = F // ft
    cut = (n_tiles + 1) // 2 * ft
    spans = ((0, cut), (cut, F - cut))
    own = [
        jnp.concatenate([gate_pre[:, a : a + f], up_pre[:, a : a + f]], axis=0) for a, f in spans
    ]

    def chunked(which):
        start, width = spans[which]
        return [(start, at, min(2 * ft, width - at)) for at in range(0, width, 2 * ft)]

    def use(chunk, pieces, pairs, total):
        start, at, f = chunk
        total, d_gate, d_up = input_grad(
            where, pieces, pairs, w_gate, w_up, keep_gate, keep_up, total, start, at, f, n_row, dt
        )
        return total, (d_gate, d_up, start + at, f)

    def weights(job, held):
        d_gate, d_up, at, f = job
        return weight_grads(tok_all, d_gate, d_up, keep_gate, keep_up, held, at, f, dt)

    def down(which, pairs, grad_down):
        start, width = spans[which]
        return down_grad(
            where, pairs, grad_all, keep_down, grad_down, start, width, n_row, ft
        )

    if n_row != 4:
        where = jnp.stack([(row - s) % n_row for s in range(n_row)]).astype(jnp.int32)
        grad_all = pair_gather(pairs_gather(out_grad, n_col), n_col, col)
        tok_all = pair_gather(pairs_gather(tokens, n_col), n_col, col)
        total = held = grad_down = None
        for which, part in enumerate(dhidden_part(grad_all, w_down, keep_down, cut, ft)):
            pairs = ring_gather(own[which], n_row)
            pieces = ring_gather(ring_reduce(part, n_row, row), n_row)
            for chunk in chunked(which):
                total, job = use(chunk, pieces, pairs, total)
                held = weights(job, held)
            grad_down = down(which, pairs, grad_down)
        grad_x = pair_reduce(pair_sums(total, n_col, col), n_col, col).astype(BF16)
        return (grad_x, held[0], held[1], grad_down)

    def after(x, *deps):
        return lax.optimization_barrier((x, *deps))[0]

    four = Four(row)
    where = four.where
    outer, inner = four.outer, four.inner
    a, b = Gather(four, own[0]), Gather(four, own[1])
    b.swap()
    a.cross()
    mine = pairs_gather(out_grad, n_col)
    grad_all = pair_gather(after(mine, b.next, a.near, keep_down), n_col, col)
    a.swap()
    b.cross()
    low, high = dhidden_part(grad_all, w_down, keep_down, cut, ft)
    sum_a, sum_b = Reduce(four, low), Reduce(four, high)
    inner.hold(high)
    a.cross_next()
    a.spread(sum_a.others().astype(BF16))
    tok_mine = pairs_gather(after(tokens, a.far), n_col, True)
    b.spread(sum_b.others().astype(BF16))
    sum_a.cross(a.near_out)
    a.spread_next()
    sum_b.cross(b.near_out)
    outer.hold(a.far_out)
    sum_a.swap()
    b.cross_next()
    grad_down = down(0, a.pieces(), None)
    sum_b.swap()
    tok_all = pair_gather(tok_mine, n_col, col)
    h_a = Gather(four, sum_a.result())
    inner.hold(grad_down)
    h_a.cross()
    h_a.swap()
    outer.hold(tok_all)
    h_a.spread()
    h_a.cross_next()
    h_b = Gather(four, sum_b.result())
    h_b.cross()
    h_a.spread_next()
    h_b.swap()
    b.spread_next()
    h_b.cross_next()
    total = held = None
    first, second = chunked(0), chunked(1)
    jobs = []
    later = [h_b.spread, h_b.spread_next]
    for c in first:
        total, job = use(c, h_a.pieces(), a.pieces(), total)
        jobs.append(job)
        outer.hold(total)
        if later:
            later.pop(0)()
    for step in later:
        step()
    for job in jobs:
        held = weights(job, held)
    total = after(total, held[0])
    jobs = []
    for c in second:
        total, job = use(c, h_b.pieces(), b.pieces(), total)
        jobs.append(job)
    summed = pair_sums(total, n_col, col)
    held = weights(jobs[0], held)
    grad_x = pair_reduce(summed, n_col, col).astype(BF16)
    for job in jobs[1:]:
        held = weights((after(job[0], summed), *job[1:]), held)
    pieces = b.pieces()
    pieces[0] = after(pieces[0], summed)
    grad_down = down(1, pieces, grad_down)
    return (grad_x, held[0], held[1], grad_down)


def solution(mesh):
    return jax.shard_map(
        functools.partial(per_device, mesh.shape["row"], mesh.shape["col"]),
        mesh=mesh,
        in_specs=(
            P("col", "row"),
            P("col", "row"),
            P("row", "col"),
            P("row", "col"),
            P("row", "col"),
            P("row", "col"),
            P("col", "row"),
            P("row", "col"),
            P("row", "col"),
            P("col", "row"),
        ),
        out_specs=(P("col", "row"), P("row", "col"), P("row", "col"), P("col", "row")),
        check_vma=False,
    )
```

```python
import functools

import jax
import jax.numpy as jnp
from jax import lax
from jax.experimental import pallas as pl
from jax.experimental.pallas import tpu as pltpu
from jax.sharding import PartitionSpec as P

TILE = 64
VMEM_LIMIT = 56 * 1024 * 1024
BF16, F32 = jnp.bfloat16, jnp.float32


def params(n_axes=1):
    return pltpu.CompilerParams(
        dimension_semantics=("arbitrary",) * n_axes, vmem_limit_bytes=VMEM_LIMIT
    )


def whole(shape):
    return pl.BlockSpec(shape, lambda j, *_: (0,) * len(shape))


def masked(block, keep):
    rows = [
        block[r * TILE : (r + 1) * TILE] * keep[r : r + 1] for r in range(keep.shape[0])
    ]
    return jnp.concatenate(rows, axis=0)


def dhidden_kernel(grad_ref, w_ref, keep_ref, out_ref):
    w_eff = masked(w_ref[...], keep_ref[0].astype(BF16))
    out_ref[...] = lax.dot_general(
        grad_ref[...], w_eff, (((1,), (1,)), ((), ())), preferred_element_type=F32
    )


def dhidden_part(grad_all, w_down, keep_down, span, ft):
    T, D = grad_all.shape
    start, width = span
    here = start // ft
    return pl.pallas_call(
        dhidden_kernel,
        out_shape=jax.ShapeDtypeStruct((T, width), F32),
        grid=(width // ft,),
        in_specs=[
            whole((T, D)),
            pl.BlockSpec((ft, D), lambda j: (j + here, 0)),
            pl.BlockSpec((1, ft // TILE, D), lambda j: (j + here, 0, 0)),
        ],
        out_specs=pl.BlockSpec((T, ft), lambda j: (0, j)),
        compiler_params=params(),
        cost_estimate=pl.CostEstimate(
            flops=2 * T * D * width,
            bytes_accessed=2 * D * width + 4 * T * width,
            transcendentals=0,
        ),
        name="dhidden",
    )(grad_all, w_down, keep_down)


def in_order(at_ref, buf, pieces, rows, half=0):
    for s, piece in enumerate(pieces):
        start = pl.multiple_of(at_ref[s] * rows, 16)
        buf[pl.ds(start, rows), :] = piece[half * rows : (half + 1) * rows, :]
    return buf[: buf.shape[0] - rows, :]


def gate_parts(gate, up):
    gate_val, up_val = gate.astype(F32), up.astype(F32)
    sig = jax.nn.sigmoid(gate_val)
    return gate_val, up_val, sig, gate_val * sig


def down_kernel(n, rows, at_ref, *refs):
    pairs, refs = refs[:n], refs[n:]
    grad_ref, keep_ref = refs[:2]
    gdown_ref, buf = refs[-2:]
    gate = in_order(at_ref, buf, pairs, rows, 0)
    up = in_order(at_ref, buf, pairs, rows, 1)
    _, up_val, _, silu = gate_parts(gate, up)
    hidden = (silu * up_val).astype(BF16)
    out = lax.dot_general(
        hidden, grad_ref[...], (((0,), (0,)), ((), ())), preferred_element_type=F32
    )
    gdown_ref[...] = masked(out, keep_ref[0]).astype(BF16)


def down_grad(where, pairs, grad_all, keep_down, held, at, f, n_row, ft):
    T, D = grad_all.shape
    F = keep_down.shape[0] * ft
    rows, n = pairs[0].shape[0], len(pairs)
    first = held is None
    args = [where, *pairs, grad_all, keep_down]
    here = at // ft
    return pl.pallas_call(
        functools.partial(down_kernel, n, rows // 2),
        out_shape=jax.ShapeDtypeStruct((F, D), BF16),
        grid_spec=pltpu.PrefetchScalarGridSpec(
            num_scalar_prefetch=1,
            grid=(f // ft,),
            in_specs=[pl.BlockSpec((rows, ft), lambda j, *_: (0, j))] * n
            + [whole((T, D)), pl.BlockSpec((1, ft // TILE, D), lambda j, *_: (j + here, 0, 0))]
            + ([] if first else [pl.BlockSpec(memory_space=pl.ANY)]),
            out_specs=pl.BlockSpec((ft, D), lambda j, *_: (j + here, 0)),
            scratch_shapes=[pltpu.VMEM(((n_row + 1) * rows // 2, ft), BF16)],
        ),
        input_output_aliases={} if first else {len(args): 0},
        compiler_params=params(),
        cost_estimate=pl.CostEstimate(
            flops=2 * T * D * f, bytes_accessed=2 * D * f + 14 * T * f, transcendentals=T * f
        ),
        name="grad_down",
    )(*args, *([] if first else [held]))


def input_kernel(n, rows, first, at_ref, *refs):
    pieces, pairs, rest = refs[:n], refs[n : 2 * n], refs[2 * n :]
    wg_ref, wu_ref, kg_ref, ku_ref = rest[:4]
    rest = rest[4:]
    if not first:
        sum_ref, rest = rest[0], rest[1:]
    gx_ref, dg_ref, du_ref, buf, dg_all, du_all = rest
    c = pl.program_id(1)

    @pl.when(pl.program_id(0) == 0)
    def _():
        d_hidden = in_order(at_ref, buf, pieces, rows).astype(F32)
        gate = in_order(at_ref, buf, pairs, rows, 0)
        up = in_order(at_ref, buf, pairs, rows, 1)
        gate_val, up_val, sig, silu = gate_parts(gate, up)
        d_gate = (d_hidden * up_val * sig * (1.0 + gate_val * (1.0 - sig))).astype(BF16)
        d_up = (d_hidden * silu).astype(BF16)
        dg_ref[...] = d_gate
        du_ref[...] = d_up
        dg_all[c] = d_gate
        du_all[c] = d_up

    dims = (((1,), (1,)), ((), ()))
    wg = masked(wg_ref[...], kg_ref[...].astype(BF16))
    wu = masked(wu_ref[...], ku_ref[...].astype(BF16))
    out = lax.dot_general(dg_all[c], wg, dims, preferred_element_type=F32)
    out = out + lax.dot_general(du_all[c], wu, dims, preferred_element_type=F32)

    @pl.when(c == 0)
    def _():
        gx_ref[...] = out if first else sum_ref[...] + out

    @pl.when(c > 0)
    def _():
        gx_ref[...] += out


def input_grad(where, pieces, pairs, w_gate, w_up, keep_gate, keep_up, total, span, n_row, ft, dt):
    rows, n = pieces[0].shape[0], len(pieces)
    T = rows * n_row
    D = w_gate.shape[0]
    start, width = span
    here, chunks = start // ft, width // ft
    first = total is None

    def once(d, c):
        return jnp.where(d == 0, c, chunks - 1)

    piece = pl.BlockSpec((rows, ft), lambda d, c, *_: (0, once(d, c)))
    pair = pl.BlockSpec((2 * rows, ft), lambda d, c, *_: (0, once(d, c)))
    tall = pl.BlockSpec((T, ft), lambda d, c, *_: (0, once(d, c)))
    weight = pl.BlockSpec((dt, ft), lambda d, c, *_: (d, c + here))
    keep = pl.BlockSpec((dt // TILE, ft), lambda d, c, *_: (d, c + here))
    gx = pl.BlockSpec((T, dt), lambda d, c, *_: (0, d))
    args = [where, *pieces, *pairs, w_gate, w_up, keep_gate, keep_up]
    return pl.pallas_call(
        functools.partial(input_kernel, n, rows, first),
        out_shape=(
            jax.ShapeDtypeStruct((T, D), F32),
            jax.ShapeDtypeStruct((T, width), BF16),
            jax.ShapeDtypeStruct((T, width), BF16),
        ),
        grid_spec=pltpu.PrefetchScalarGridSpec(
            num_scalar_prefetch=1,
            grid=(D // dt, chunks),
            in_specs=[piece] * n + [pair] * n + [weight, weight, keep, keep] + ([] if first else [gx]),
            out_specs=[gx, tall, tall],
            scratch_shapes=[
                pltpu.VMEM(((n_row + 1) * rows, ft), BF16),
                pltpu.VMEM((chunks, T, ft), BF16),
                pltpu.VMEM((chunks, T, ft), BF16),
            ],
        ),
        input_output_aliases={} if first else {len(args): 0},
        compiler_params=params(2),
        cost_estimate=pl.CostEstimate(
            flops=4 * T * D * width, bytes_accessed=4 * D * width + 8 * T * D, transcendentals=T * width
        ),
        name="grad_x_part",
    )(*args, *([] if first else [total]))


def weight_kernel(tok_ref, dg_ref, du_ref, kg_ref, ku_ref, *refs):
    gg_ref, gu_ref = refs[-2:]
    tok = tok_ref[...]
    dims = (((0,), (0,)), ((), ()))
    gg = lax.dot_general(tok, dg_ref[...], dims, preferred_element_type=F32)
    gg_ref[...] = masked(gg, kg_ref[...]).astype(BF16)
    gu = lax.dot_general(tok, du_ref[...], dims, preferred_element_type=F32)
    gu_ref[...] = masked(gu, ku_ref[...]).astype(BF16)


def weight_grads(tok_all, d_gate, d_up, keep_gate, keep_up, held, span, part, ft):
    T, D = tok_all.shape
    F = keep_gate.shape[1]
    at, width = part[0] // ft, part[1]
    here = span[0] // ft + at
    keep = pl.BlockSpec((D // TILE, ft), lambda c: (0, c + here))
    out = pl.BlockSpec((D, ft), lambda c: (0, c + here))
    tall = pl.BlockSpec((T, ft), lambda c: (0, c + at))
    return pl.pallas_call(
        weight_kernel,
        out_shape=(jax.ShapeDtypeStruct((D, F), BF16),) * 2,
        grid=(width // ft,),
        in_specs=[whole((T, D)), tall, tall, keep, keep]
        + ([] if held is None else [pl.BlockSpec(memory_space=pl.ANY)] * 2),
        out_specs=[out, out],
        input_output_aliases={} if held is None else {5: 0, 6: 1},
        compiler_params=params(),
        cost_estimate=pl.CostEstimate(
            flops=4 * T * D * width, bytes_accessed=4 * D * width + 2 * T * D, transcendentals=0
        ),
        name="grad_gate_up",
    )(tok_all, d_gate, d_up, keep_gate, keep_up, *([] if held is None else held))


class Queue:
    def __init__(self, perm):
        self.perm, self.flying = perm, [(), ()]

    def hold(self, *deps):
        self.flying[0] = (*self.flying[0], *deps)

    def issue(self, x):
        wait = self.flying.pop(0)
        if wait:
            x, *_ = lax.optimization_barrier((x, *wait))
        x = lax.ppermute(x, "row", self.perm)
        self.flying.append((x,))
        return x


class Four:
    def __init__(self, me):
        self.me = me
        self.outer = Queue([(0, 1), (1, 0), (2, 3), (3, 2)])
        self.inner = Queue([(1, 2), (2, 1)])
        self.mid = (me == 1) | (me == 2)
        self.side = me // 2
        near, far = jnp.where(self.side == 0, 2, 1), jnp.where(self.side == 0, 3, 0)
        self.where = jnp.stack(
            [
                me,
                me ^ 1,
                jnp.where(self.mid, near, 4),
                jnp.where(self.mid, far, 4),
                jnp.where(self.mid, 4, near),
                jnp.where(self.mid, 4, far),
            ]
        ).astype(jnp.int32)


class Gather:
    def __init__(self, four, piece):
        self.four, self.own = four, piece

    def swap(self):
        self.next = self.four.outer.issue(self.own)

    def cross(self):
        self.near = self.four.inner.issue(self.own)

    def cross_next(self):
        self.far = self.four.inner.issue(self.next)

    def spread(self, outwards=None):
        send = self.near if outwards is None else jnp.where(self.four.mid, self.near, outwards)
        self.near_out = self.four.outer.issue(send)

    def spread_next(self):
        self.far_out = self.four.outer.issue(self.far)

    def pieces(self):
        return [self.own, self.next, self.near, self.far, self.near_out, self.far_out]


class Reduce:
    def __init__(self, four, part):
        self.four, self.part = four, part
        self.rows = part.shape[0] // 4

    def block(self, b, count=1):
        return lax.dynamic_slice_in_dim(self.part, b * self.rows, count * self.rows, 0)

    def others(self):
        return self.block(2 - 2 * self.four.side, 2)

    def cross(self, from_end):
        send = (self.others() + from_end.astype(F32)).astype(BF16)
        self.crossed = self.four.inner.issue(send)

    def crossed_block(self, b):
        got = lax.dynamic_slice_in_dim(self.crossed, (b % 2) * self.rows, self.rows, 0)
        return jnp.where(self.four.mid, got.astype(F32), 0.0)

    def swap(self):
        other = self.four.me ^ 1
        self.swapped = self.four.outer.issue(
            (self.block(other) + self.crossed_block(other)).astype(BF16)
        )

    def result(self):
        me = self.four.me
        return (self.block(me) + self.crossed_block(me) + self.swapped.astype(F32)).astype(BF16)


def ring_gather(piece, n):
    ring = [(i, (i + 1) % n) for i in range(n)]
    pieces = [piece]
    for _ in range(1, n):
        pieces.append(lax.ppermute(pieces[-1], "row", ring))
    return pieces


def ring_reduce(part, n, me):
    ring = [(i, (i + 1) % n) for i in range(n)]
    rows = part.shape[0] // n
    total = None
    for s in range(n):
        block = lax.dynamic_slice_in_dim(part, (me + n - 1 - s) % n * rows, rows, 0)
        total = block if total is None else block + total.astype(F32)
        total = total.astype(BF16)
        if s < n - 1:
            total = lax.ppermute(total, "row", ring)
    return total


def pairs_gather(piece, n, in_turn=False):
    got = [piece]
    for k in range(1, n // 2):
        send = lax.optimization_barrier((piece, got[-1]))[0] if in_turn else piece
        got.append(lax.ppermute(send, "col", [(i, i ^ (2 * k)) for i in range(n)]))
    return jnp.stack(got)


def pair_gather(mine, n, me):
    half, rows, width = mine.shape
    core, pair = me % 2, me // 2
    other = lax.ppermute(mine, "col", [(i, i ^ 1) for i in range(n)])
    even, odd = jnp.where(core == 0, mine, other), jnp.where(core == 0, other, mine)
    both = jnp.stack([even, odd], axis=1)
    ordered = [lax.dynamic_index_in_dim(both, pair ^ k, 0, keepdims=False) for k in range(half)]
    return jnp.stack(ordered).reshape(n * rows, width)


def pair_sums(part, n, me):
    rows = part.shape[0] // n
    core = me % 2
    blocks = part.reshape(n // 2, 2, rows, part.shape[1])
    send = lax.dynamic_index_in_dim(blocks, 1 - core, 1, keepdims=False)
    keep = lax.dynamic_index_in_dim(blocks, core, 1, keepdims=False)
    return keep + lax.ppermute(send, "col", [(i, i ^ 1) for i in range(n)])


def pair_reduce(summed, n, me):
    half = n // 2
    pair = me // 2
    total = lax.dynamic_index_in_dim(summed, pair, 0, keepdims=False)
    low = summed.astype(BF16)
    got = [
        lax.ppermute(
            lax.dynamic_index_in_dim(low, pair ^ k, 0, keepdims=False),
            "col",
            [(i, i ^ (2 * k)) for i in range(n)],
        )
        for k in range(1, half)
    ]
    for g in got:
        total = total + g.astype(F32)
    return total


def lanes(mask):
    return jnp.repeat(mask.astype(F32), TILE, axis=1)


def per_device(
    n_row,
    n_col,
    tokens,
    out_grad,
    gate_pre,
    up_pre,
    w_gate,
    w_up,
    w_down,
    mask_gate,
    mask_up,
    mask_down,
):
    row, col = lax.axis_index("row"), lax.axis_index("col")
    F, D = w_down.shape
    ft = 512 if F % 512 == 0 else 256
    dt = min(1024, D)
    keep_gate, keep_up, keep_down = lanes(mask_gate), lanes(mask_up), lanes(mask_down)
    keep_down = keep_down.reshape(F // ft, ft // TILE, D)

    n_tiles = F // ft
    cut = (n_tiles + 1) // 2 * ft
    spans = ((0, cut), (cut, F - cut))
    own = [
        jnp.concatenate([gate_pre[:, a : a + f], up_pre[:, a : a + f]], axis=0) for a, f in spans
    ]

    def use(which, pieces, pairs, total):
        return input_grad(
            where, pieces, pairs, w_gate, w_up, keep_gate, keep_up, total, spans[which], n_row, ft, dt
        )

    def weights(which, d_gate, d_up, held, part=None):
        span = spans[which]
        part = part or (0, span[1])
        return weight_grads(tok_all, d_gate, d_up, keep_gate, keep_up, held, span, part, ft)

    def down(which, pairs, grad_down):
        start, width = spans[which]
        return down_grad(
            where, pairs, grad_all, keep_down, grad_down, start, width, n_row, ft
        )

    if n_row != 4:
        where = jnp.stack([(row - s) % n_row for s in range(n_row)]).astype(jnp.int32)
        grad_all = pair_gather(pairs_gather(out_grad, n_col), n_col, col)
        tok_all = pair_gather(pairs_gather(tokens, n_col), n_col, col)
        total = held = grad_down = None
        for which, span in enumerate(spans):
            part = dhidden_part(grad_all, w_down, keep_down, span, ft)
            pairs = ring_gather(own[which], n_row)
            pieces = ring_gather(ring_reduce(part, n_row, row), n_row)
            total, d_gate, d_up = use(which, pieces, pairs, total)
            held = weights(which, d_gate, d_up, held)
            grad_down = down(which, pairs, grad_down)
        grad_x = pair_reduce(pair_sums(total, n_col, col), n_col, col).astype(BF16)
        return (grad_x, held[0], held[1], grad_down)

    def after(x, *deps):
        return lax.optimization_barrier((x, *deps))[0]

    four = Four(row)
    where = four.where
    outer, inner = four.outer, four.inner
    a, b = Gather(four, own[0]), Gather(four, own[1])
    a.swap()
    a.cross()
    mine = pairs_gather(out_grad, n_col)
    grad_all = pair_gather(after(mine, a.next, a.near, keep_down), n_col, col)
    b.swap()
    b.cross()
    low = dhidden_part(grad_all, w_down, keep_down, spans[0], ft)
    sum_a = Reduce(four, low)
    outwards = sum_a.others().astype(BF16)
    outer.hold(b.next, b.near)
    a.spread(outwards)
    sum_b = Reduce(four, dhidden_part(grad_all, w_down, keep_down, spans[1], ft))
    inner.hold(outwards)
    a.cross_next()
    tok_mine = pairs_gather(after(tokens, a.far), n_col, True)
    b_outwards = sum_b.others().astype(BF16)
    b.spread(b_outwards)
    inner.hold(b_outwards)
    sum_a.cross(a.near_out)
    outer.hold(b.near_out)
    a.spread_next()
    b.cross_next()
    sum_b.cross(b.near_out)
    outer.hold(a.far_out, b.far)
    sum_a.swap()
    tok_all = pair_gather(tok_mine, n_col, col)
    h_a = Gather(four, sum_a.result())
    h_a.cross()
    h_a.swap()
    sum_b.swap()
    grad_down = down(0, a.pieces(), None)
    inner.hold(grad_down, h_a.near)
    h_a.spread()
    h_a.cross_next()
    h_b = Gather(four, sum_b.result())
    h_b.cross()
    outer.hold(h_a.near_out)
    h_a.spread_next()
    outer.hold(tok_all)
    h_b.swap()
    b.spread_next()
    total, d_gate, d_up = use(0, h_a.pieces(), a.pieces(), None)
    inner.hold(total)
    h_b.cross_next()
    outer.hold(total)
    h_b.spread()
    half = cut // ft // 2 * ft
    held = weights(0, d_gate, d_up, None, (0, half))
    outer.hold(held[0])
    h_b.spread_next()
    held = weights(0, d_gate, d_up, held, (half, cut - half))
    total = after(total, held[0])
    total, d_gate, d_up = use(1, h_b.pieces(), b.pieces(), total)
    summed = pair_sums(total, n_col, col)
    grad_down = down(1, b.pieces(), grad_down)
    grad_x = pair_reduce(summed, n_col, col).astype(BF16)
    held = weights(1, after(d_gate, summed), d_up, held)
    return (grad_x, held[0], held[1], grad_down)


def solution(mesh):
    return jax.shard_map(
        functools.partial(per_device, mesh.shape["row"], mesh.shape["col"]),
        mesh=mesh,
        in_specs=(
            P("col", "row"),
            P("col", "row"),
            P("row", "col"),
            P("row", "col"),
            P("row", "col"),
            P("row", "col"),
            P("col", "row"),
            P("row", "col"),
            P("row", "col"),
            P("col", "row"),
        ),
        out_specs=(P("col", "row"), P("row", "col"), P("row", "col"), P("col", "row")),
        check_vma=False,
    )
```

```python
import functools

import jax
import jax.numpy as jnp
from jax import lax
from jax.experimental import pallas as pl
from jax.experimental.pallas import tpu as pltpu
from jax.sharding import PartitionSpec as P

TILE = 64
VMEM_LIMIT = 56 * 1024 * 1024
BF16, F32 = jnp.bfloat16, jnp.float32


def params(n_axes=1):
    return pltpu.CompilerParams(
        dimension_semantics=("arbitrary",) * n_axes, vmem_limit_bytes=VMEM_LIMIT
    )


def whole(shape):
    return pl.BlockSpec(shape, lambda j, *_: (0,) * len(shape))


def masked(block, keep):
    rows = [
        block[r * TILE : (r + 1) * TILE] * keep[r : r + 1] for r in range(keep.shape[0])
    ]
    return jnp.concatenate(rows, axis=0)


def dhidden_kernel(grad_ref, w_ref, keep_ref, out_ref):
    w_eff = masked(w_ref[...], keep_ref[0].astype(BF16))
    out_ref[...] = lax.dot_general(
        grad_ref[...], w_eff, (((1,), (1,)), ((), ())), preferred_element_type=F32
    )


def dhidden_part(grad_all, w_down, keep_down, span, ft):
    T, D = grad_all.shape
    start, width = span
    here = start // ft
    return pl.pallas_call(
        dhidden_kernel,
        out_shape=jax.ShapeDtypeStruct((T, width), F32),
        grid=(width // ft,),
        in_specs=[
            whole((T, D)),
            pl.BlockSpec((ft, D), lambda j: (j + here, 0)),
            pl.BlockSpec((1, ft // TILE, D), lambda j: (j + here, 0, 0)),
        ],
        out_specs=pl.BlockSpec((T, ft), lambda j: (0, j)),
        compiler_params=params(),
        cost_estimate=pl.CostEstimate(
            flops=2 * T * D * width,
            bytes_accessed=2 * D * width + 4 * T * width,
            transcendentals=0,
        ),
        name="dhidden",
    )(grad_all, w_down, keep_down)


def in_order(at_ref, buf, pieces, rows, half=0):
    for s, piece in enumerate(pieces):
        start = pl.multiple_of(at_ref[s] * rows, 16)
        buf[pl.ds(start, rows), :] = piece[half * rows : (half + 1) * rows, :]
    return buf[: buf.shape[0] - rows, :]


def gate_parts(gate, up):
    gate_val, up_val = gate.astype(F32), up.astype(F32)
    sig = jax.nn.sigmoid(gate_val)
    return gate_val, up_val, sig, gate_val * sig


def down_kernel(n, rows, factors, at_ref, *refs):
    pairs, refs = refs[:n], refs[n:]
    grad_ref, keep_ref = refs[:2]
    buf, outs = refs[-1], refs[:-1]
    gdown_ref = outs[-3] if factors else outs[-1]
    gate = in_order(at_ref, buf, pairs, rows, 0)
    up = in_order(at_ref, buf, pairs, rows, 1)
    gate_val, up_val, sig, silu = gate_parts(gate, up)
    if factors:
        outs[-2][...] = up_val * sig * (1.0 + gate_val * (1.0 - sig))
        outs[-1][...] = silu
    hidden = (silu * up_val).astype(BF16)
    out = lax.dot_general(
        hidden, grad_ref[...], (((0,), (0,)), ((), ())), preferred_element_type=F32
    )
    gdown_ref[...] = masked(out, keep_ref[0]).astype(BF16)


def down_grad(where, pairs, grad_all, keep_down, held, at, f, n_row, ft, factors=False):
    T, D = grad_all.shape
    F = keep_down.shape[0] * ft
    rows, n = pairs[0].shape[0], len(pairs)
    first = held is None
    args = [where, *pairs, grad_all, keep_down]
    here = at // ft
    return pl.pallas_call(
        functools.partial(down_kernel, n, rows // 2, factors),
        out_shape=[jax.ShapeDtypeStruct((F, D), BF16)]
        + ([jax.ShapeDtypeStruct((T, f), F32)] * 2 if factors else []),
        grid_spec=pltpu.PrefetchScalarGridSpec(
            num_scalar_prefetch=1,
            grid=(f // ft,),
            in_specs=[pl.BlockSpec((rows, ft), lambda j, *_: (0, j))] * n
            + [whole((T, D)), pl.BlockSpec((1, ft // TILE, D), lambda j, *_: (j + here, 0, 0))]
            + ([] if first else [pl.BlockSpec(memory_space=pl.ANY)]),
            out_specs=[pl.BlockSpec((ft, D), lambda j, *_: (j + here, 0))]
            + ([pl.BlockSpec((T, ft), lambda j, *_: (0, j))] * 2 if factors else []),
            scratch_shapes=[pltpu.VMEM(((n_row + 1) * rows // 2, ft), BF16)],
        ),
        input_output_aliases={} if first else {len(args): 0},
        compiler_params=params(),
        cost_estimate=pl.CostEstimate(
            flops=2 * T * D * f, bytes_accessed=2 * D * f + 14 * T * f, transcendentals=T * f
        ),
        name="grad_down",
    )(*args, *([] if first else [held]))


def input_kernel(n, rows, n_pair, first, last, at_ref, *refs):
    pieces, refs = refs[:n], refs[n:]
    pairs, rest = refs[:n_pair], refs[n_pair:]
    wg_ref, wu_ref, kg_ref, ku_ref = rest[:4]
    rest = rest[4:]
    if not first:
        sum_ref, rest = rest[0], rest[1:]
    gx_ref, dg_ref, du_ref = rest[:3]
    buf, dg_all, du_all = rest[-3:]
    c = pl.program_id(1)

    @pl.when(pl.program_id(0) == 0)
    def _():
        d_hidden = in_order(at_ref, buf, pieces, rows).astype(F32)
        if n_pair == 2:
            d_gate = (d_hidden * pairs[0][...]).astype(BF16)
            d_up = (d_hidden * pairs[1][...]).astype(BF16)
        else:
            gate = in_order(at_ref, buf, pairs, rows, 0)
            up = in_order(at_ref, buf, pairs, rows, 1)
            gate_val, up_val, sig, silu = gate_parts(gate, up)
            d_gate = (d_hidden * up_val * sig * (1.0 + gate_val * (1.0 - sig))).astype(BF16)
            d_up = (d_hidden * silu).astype(BF16)
        dg_ref[...] = d_gate
        du_ref[...] = d_up
        dg_all[c] = d_gate
        du_all[c] = d_up

    dims = (((1,), (1,)), ((), ()))
    wg = masked(wg_ref[...], kg_ref[...].astype(BF16))
    wu = masked(wu_ref[...], ku_ref[...].astype(BF16))
    out = lax.dot_general(dg_all[c], wg, dims, preferred_element_type=F32)
    out = out + lax.dot_general(du_all[c], wu, dims, preferred_element_type=F32)

    @pl.when(c == 0)
    def _():
        gx_ref[...] = out if first else sum_ref[...] + out

    @pl.when(c > 0)
    def _():
        gx_ref[...] += out

    if last:

        @pl.when(c == pl.num_programs(1) - 1)
        def _():
            send_ref = rest[3]
            per = last
            for p in range(send_ref.shape[0] // per):
                start = pl.multiple_of((2 * p + 1 - at_ref[n]) * per, 8)
                send_ref[p * per : (p + 1) * per, :] = gx_ref[pl.ds(start, per), :]


def input_grad(where, pieces, pairs, w_gate, w_up, keep_gate, keep_up, total, span, last, n_row, ft, dt):
    rows, n = pieces[0].shape[0], len(pieces)
    T = rows * n_row
    D = w_gate.shape[0]
    start, width = span
    here, chunks = start // ft, width // ft
    first = total is None

    def once(d, c):
        return jnp.where(d == 0, c, chunks - 1)

    piece = pl.BlockSpec((rows, ft), lambda d, c, *_: (0, once(d, c)))
    pair = pl.BlockSpec((pairs[0].shape[0], ft), lambda d, c, *_: (0, once(d, c)))
    tall = pl.BlockSpec((T, ft), lambda d, c, *_: (0, once(d, c)))
    weight = pl.BlockSpec((dt, ft), lambda d, c, *_: (d, c + here))
    keep = pl.BlockSpec((dt // TILE, ft), lambda d, c, *_: (d, c + here))
    gx = pl.BlockSpec((T, dt), lambda d, c, *_: (0, d))
    args = [where, *pieces, *pairs, w_gate, w_up, keep_gate, keep_up]
    return pl.pallas_call(
        functools.partial(input_kernel, n, rows, len(pairs), first, last),
        out_shape=[
            jax.ShapeDtypeStruct((T, D), F32),
            jax.ShapeDtypeStruct((T, width), BF16),
            jax.ShapeDtypeStruct((T, width), BF16),
        ]
        + ([jax.ShapeDtypeStruct((T // 2, D), F32)] if last else []),
        grid_spec=pltpu.PrefetchScalarGridSpec(
            num_scalar_prefetch=1,
            grid=(D // dt, chunks),
            in_specs=[piece] * n
            + [pair] * len(pairs)
            + [weight, weight, keep, keep]
            + ([] if first else [gx]),
            out_specs=[gx, tall, tall]
            + ([pl.BlockSpec((T // 2, dt), lambda d, c, *_: (0, d))] if last else []),
            scratch_shapes=[
                pltpu.VMEM(((n_row + 1) * rows, ft), BF16),
                pltpu.VMEM((chunks, T, ft), BF16),
                pltpu.VMEM((chunks, T, ft), BF16),
            ],
        ),
        input_output_aliases={} if first else {len(args): 0},
        compiler_params=params(2),
        cost_estimate=pl.CostEstimate(
            flops=4 * T * D * width, bytes_accessed=4 * D * width + 8 * T * D, transcendentals=T * width
        ),
        name="grad_x_part",
    )(*args, *([] if first else [total]))


def weight_kernel(tok_ref, dg_ref, du_ref, kg_ref, ku_ref, *refs):
    gg_ref, gu_ref = refs[-2:]
    tok = tok_ref[...]
    dims = (((0,), (0,)), ((), ()))
    gg = lax.dot_general(tok, dg_ref[...], dims, preferred_element_type=F32)
    gg_ref[...] = masked(gg, kg_ref[...]).astype(BF16)
    gu = lax.dot_general(tok, du_ref[...], dims, preferred_element_type=F32)
    gu_ref[...] = masked(gu, ku_ref[...]).astype(BF16)


def weight_grads(tok_all, d_gate, d_up, keep_gate, keep_up, held, span, part, ft):
    T, D = tok_all.shape
    F = keep_gate.shape[1]
    at, width = part[0] // ft, part[1]
    here = span[0] // ft + at
    keep = pl.BlockSpec((D // TILE, ft), lambda c: (0, c + here))
    out = pl.BlockSpec((D, ft), lambda c: (0, c + here))
    tall = pl.BlockSpec((T, ft), lambda c: (0, c + at))
    return pl.pallas_call(
        weight_kernel,
        out_shape=(jax.ShapeDtypeStruct((D, F), BF16),) * 2,
        grid=(width // ft,),
        in_specs=[whole((T, D)), tall, tall, keep, keep]
        + ([] if held is None else [pl.BlockSpec(memory_space=pl.ANY)] * 2),
        out_specs=[out, out],
        input_output_aliases={} if held is None else {5: 0, 6: 1},
        compiler_params=params(),
        cost_estimate=pl.CostEstimate(
            flops=4 * T * D * width, bytes_accessed=4 * D * width + 2 * T * D, transcendentals=0
        ),
        name="grad_gate_up",
    )(tok_all, d_gate, d_up, keep_gate, keep_up, *([] if held is None else held))


class Queue:
    def __init__(self, perm):
        self.perm, self.flying = perm, [(), ()]

    def hold(self, *deps):
        self.flying[0] = (*self.flying[0], *deps)

    def issue(self, x):
        wait = self.flying.pop(0)
        if wait:
            x, *_ = lax.optimization_barrier((x, *wait))
        x = lax.ppermute(x, "row", self.perm)
        self.flying.append((x,))
        return x


class Four:
    def __init__(self, me):
        self.me = me
        self.outer = Queue([(0, 1), (1, 0), (2, 3), (3, 2)])
        self.inner = Queue([(1, 2), (2, 1)])
        self.mid = (me == 1) | (me == 2)
        self.side = me // 2
        near, far = jnp.where(self.side == 0, 2, 1), jnp.where(self.side == 0, 3, 0)
        self.where = jnp.stack(
            [
                me,
                me ^ 1,
                jnp.where(self.mid, near, 4),
                jnp.where(self.mid, far, 4),
                jnp.where(self.mid, 4, near),
                jnp.where(self.mid, 4, far),
            ]
        ).astype(jnp.int32)


class Gather:
    def __init__(self, four, piece):
        self.four, self.own = four, piece

    def swap(self):
        self.next = self.four.outer.issue(self.own)

    def cross(self):
        self.near = self.four.inner.issue(self.own)

    def cross_next(self):
        self.far = self.four.inner.issue(self.next)

    def spread(self, outwards=None):
        send = self.near if outwards is None else jnp.where(self.four.mid, self.near, outwards)
        self.near_out = self.four.outer.issue(send)

    def spread_next(self):
        self.far_out = self.four.outer.issue(self.far)

    def pieces(self):
        return [self.own, self.next, self.near, self.far, self.near_out, self.far_out]


class Reduce:
    def __init__(self, four, part):
        self.four, self.part = four, part
        self.rows = part.shape[0] // 4

    def block(self, b, count=1):
        return lax.dynamic_slice_in_dim(self.part, b * self.rows, count * self.rows, 0)

    def others(self):
        return self.block(2 - 2 * self.four.side, 2)

    def cross(self, from_end):
        send = (self.others() + from_end.astype(F32)).astype(BF16)
        self.crossed = self.four.inner.issue(send)

    def crossed_block(self, b):
        got = lax.dynamic_slice_in_dim(self.crossed, (b % 2) * self.rows, self.rows, 0)
        return jnp.where(self.four.mid, got.astype(F32), 0.0)

    def swap(self):
        other = self.four.me ^ 1
        self.swapped = self.four.outer.issue(
            (self.block(other) + self.crossed_block(other)).astype(BF16)
        )

    def result(self):
        me = self.four.me
        return (self.block(me) + self.crossed_block(me) + self.swapped.astype(F32)).astype(BF16)


def ring_gather(piece, n):
    ring = [(i, (i + 1) % n) for i in range(n)]
    pieces = [piece]
    for _ in range(1, n):
        pieces.append(lax.ppermute(pieces[-1], "row", ring))
    return pieces


def ring_reduce(part, n, me):
    ring = [(i, (i + 1) % n) for i in range(n)]
    rows = part.shape[0] // n
    total = None
    for s in range(n):
        block = lax.dynamic_slice_in_dim(part, (me + n - 1 - s) % n * rows, rows, 0)
        total = block if total is None else block + total.astype(F32)
        total = total.astype(BF16)
        if s < n - 1:
            total = lax.ppermute(total, "row", ring)
    return total


def pairs_gather(piece, n, in_turn=False):
    got = [piece]
    for k in range(1, n // 2):
        send = lax.optimization_barrier((piece, got[-1]))[0] if in_turn else piece
        got.append(lax.ppermute(send, "col", [(i, i ^ (2 * k)) for i in range(n)]))
    return jnp.stack(got)


def pair_gather(mine, n, me):
    half, rows, width = mine.shape
    core, pair = me % 2, me // 2
    other = lax.ppermute(mine, "col", [(i, i ^ 1) for i in range(n)])
    even, odd = jnp.where(core == 0, mine, other), jnp.where(core == 0, other, mine)
    both = jnp.stack([even, odd], axis=1)
    ordered = [lax.dynamic_index_in_dim(both, pair ^ k, 0, keepdims=False) for k in range(half)]
    return jnp.stack(ordered).reshape(n * rows, width)


def pair_sums(part, send, n, me):
    rows = part.shape[0] // n
    core = me % 2
    blocks = part.reshape(n // 2, 2, rows, part.shape[1])
    send = send.reshape(n // 2, rows, part.shape[1])
    keep = lax.dynamic_index_in_dim(blocks, core, 1, keepdims=False)
    return keep + lax.ppermute(send, "col", [(i, i ^ 1) for i in range(n)])


def pair_reduce(summed, n, me):
    half = n // 2
    pair = me // 2
    total = lax.dynamic_index_in_dim(summed, pair, 0, keepdims=False)
    low = summed.astype(BF16)
    got = [
        lax.ppermute(
            lax.dynamic_index_in_dim(low, pair ^ k, 0, keepdims=False),
            "col",
            [(i, i ^ (2 * k)) for i in range(n)],
        )
        for k in range(1, half)
    ]
    for g in got:
        total = total + g.astype(F32)
    return total


def lanes(mask):
    return jnp.repeat(mask.astype(F32), TILE, axis=1)


def per_device(
    n_row,
    n_col,
    tokens,
    out_grad,
    gate_pre,
    up_pre,
    w_gate,
    w_up,
    w_down,
    mask_gate,
    mask_up,
    mask_down,
):
    row, col = lax.axis_index("row"), lax.axis_index("col")
    F, D = w_down.shape
    ft = 512 if F % 512 == 0 else 256
    dt = min(2048, D)
    keep_gate, keep_up, keep_down = lanes(mask_gate), lanes(mask_up), lanes(mask_down)
    keep_down = keep_down.reshape(F // ft, ft // TILE, D)

    n_tiles = F // ft
    cut = (n_tiles + 1) // 2 * ft
    spans = ((0, cut), (cut, F - cut))
    own = [
        jnp.concatenate([gate_pre[:, a : a + f], up_pre[:, a : a + f]], axis=0) for a, f in spans
    ]

    def use(which, pieces, pairs, total):
        last = grad_all.shape[0] // n_col if which else 0
        return input_grad(
            where, pieces, pairs, w_gate, w_up, keep_gate, keep_up, total, spans[which], last, n_row, ft, dt
        )

    def weights(which, d_gate, d_up, held, part=None):
        span = spans[which]
        part = part or (0, span[1])
        return weight_grads(tok_all, d_gate, d_up, keep_gate, keep_up, held, span, part, ft)

    def down(which, pairs, grad_down, factors=False):
        start, width = spans[which]
        return down_grad(
            where, pairs, grad_all, keep_down, grad_down, start, width, n_row, ft, factors
        )

    if n_row != 4:
        where = jnp.stack([(row - s) % n_row for s in range(n_row)] + [col % 2]).astype(jnp.int32)
        grad_all = pair_gather(pairs_gather(out_grad, n_col), n_col, col)
        tok_all = pair_gather(pairs_gather(tokens, n_col), n_col, col)
        total = held = grad_down = None
        for which, span in enumerate(spans):
            part = dhidden_part(grad_all, w_down, keep_down, span, ft)
            pairs = ring_gather(own[which], n_row)
            pieces = ring_gather(ring_reduce(part, n_row, row), n_row)
            total, d_gate, d_up, *send = use(which, pieces, pairs, total)
            held = weights(which, d_gate, d_up, held)
            (grad_down,) = down(which, pairs, grad_down)
        grad_x = pair_reduce(pair_sums(total, send[0], n_col, col), n_col, col).astype(BF16)
        return (grad_x, held[0], held[1], grad_down)

    def after(x, *deps):
        return lax.optimization_barrier((x, *deps))[0]

    four = Four(row)
    where = jnp.append(four.where, (col % 2).astype(jnp.int32))
    outer, inner = four.outer, four.inner
    a, b = Gather(four, own[0]), Gather(four, own[1])
    a.swap()
    a.cross()
    mine = pairs_gather(out_grad, n_col)
    grad_all = pair_gather(after(mine, a.next, a.near, keep_down, keep_gate, keep_up), n_col, col)
    b.swap()
    b.cross()
    low = dhidden_part(grad_all, w_down, keep_down, spans[0], ft)
    sum_a = Reduce(four, low)
    outwards = sum_a.others().astype(BF16)
    outer.hold(b.next, b.near)
    a.spread(outwards)
    sum_b = Reduce(four, dhidden_part(grad_all, w_down, keep_down, spans[1], ft))
    inner.hold(outwards)
    a.cross_next()
    tok_mine = pairs_gather(after(tokens, a.far), n_col, True)
    b_outwards = sum_b.others().astype(BF16)
    b.spread(b_outwards)
    inner.hold(b_outwards)
    sum_a.cross(a.near_out)
    outer.hold(b.near_out)
    a.spread_next()
    b.cross_next()
    sum_b.cross(b.near_out)
    outer.hold(a.far_out, b.far)
    sum_a.swap()
    tok_all = pair_gather(tok_mine, n_col, col)
    h_a = Gather(four, sum_a.result())
    h_a.cross()
    h_a.swap()
    sum_b.swap()
    grad_down, *factors = down(0, a.pieces(), None, True)
    inner.hold(grad_down, h_a.near)
    h_a.spread()
    h_a.cross_next()
    h_b = Gather(four, sum_b.result())
    h_b.cross()
    outer.hold(h_a.near_out)
    h_a.spread_next()
    outer.hold(tok_all)
    h_b.swap()
    b.spread_next()
    total, d_gate, d_up = use(0, h_a.pieces(), factors, None)
    inner.hold(total)
    h_b.cross_next()
    outer.hold(total)
    h_b.spread()
    half = cut // ft // 2 * ft
    held = weights(0, d_gate, d_up, None, (0, half))
    outer.hold(held[0])
    h_b.spread_next()
    held = weights(0, d_gate, d_up, held, (half, cut - half))
    total = after(total, held[0])
    total, d_gate, d_up, send = use(1, h_b.pieces(), b.pieces(), total)
    summed = pair_sums(total, send, n_col, col)
    (grad_down,) = down(1, b.pieces(), grad_down)
    grad_x = pair_reduce(summed, n_col, col).astype(BF16)
    held = weights(1, after(d_gate, summed), d_up, held)
    return (grad_x, held[0], held[1], grad_down)


def solution(mesh):
    return jax.shard_map(
        functools.partial(per_device, mesh.shape["row"], mesh.shape["col"]),
        mesh=mesh,
        in_specs=(
            P("col", "row"),
            P("col", "row"),
            P("row", "col"),
            P("row", "col"),
            P("row", "col"),
            P("row", "col"),
            P("col", "row"),
            P("row", "col"),
            P("row", "col"),
            P("col", "row"),
        ),
        out_specs=(P("col", "row"), P("row", "col"), P("row", "col"), P("col", "row")),
        check_vma=False,
    )
```

```python
import functools

import jax
import jax.numpy as jnp
from jax import lax
from jax.experimental import pallas as pl
from jax.experimental.pallas import tpu as pltpu
from jax.sharding import PartitionSpec as P

TILE = 64
VMEM_LIMIT = 56 * 1024 * 1024
BF16, F32 = jnp.bfloat16, jnp.float32


def params(n_axes=1):
    return pltpu.CompilerParams(
        dimension_semantics=("arbitrary",) * n_axes, vmem_limit_bytes=VMEM_LIMIT
    )


def whole(shape):
    return pl.BlockSpec(shape, lambda j, *_: (0,) * len(shape))


def masked(block, keep):
    rows = [
        block[r * TILE : (r + 1) * TILE] * keep[r : r + 1] for r in range(keep.shape[0])
    ]
    return jnp.concatenate(rows, axis=0)


def dhidden_kernel(grad_ref, w_ref, keep_ref, out_ref):
    w_eff = masked(w_ref[...], keep_ref[0].astype(BF16))
    out_ref[...] = lax.dot_general(
        grad_ref[...], w_eff, (((1,), (1,)), ((), ())), preferred_element_type=F32
    )


def dhidden_part(grad_all, w_down, keep_down, span, ft):
    T, D = grad_all.shape
    start, width = span
    here = start // ft
    return pl.pallas_call(
        dhidden_kernel,
        out_shape=jax.ShapeDtypeStruct((T, width), F32),
        grid=(width // ft,),
        in_specs=[
            whole((T, D)),
            pl.BlockSpec((ft, D), lambda j: (j + here, 0)),
            pl.BlockSpec((1, ft // TILE, D), lambda j: (j + here, 0, 0)),
        ],
        out_specs=pl.BlockSpec((T, ft), lambda j: (0, j)),
        compiler_params=params(),
        cost_estimate=pl.CostEstimate(
            flops=2 * T * D * width,
            bytes_accessed=2 * D * width + 4 * T * width,
            transcendentals=0,
        ),
        name="dhidden",
    )(grad_all, w_down, keep_down)


def in_order(at_ref, buf, pieces, rows, half=0):
    for s, piece in enumerate(pieces):
        start = pl.multiple_of(at_ref[s] * rows, 16)
        buf[pl.ds(start, rows), :] = piece[half * rows : (half + 1) * rows, :]
    return buf[: buf.shape[0] - rows, :]


def gate_parts(gate, up):
    gate_val, up_val = gate.astype(F32), up.astype(F32)
    sig = jax.nn.sigmoid(gate_val)
    return gate_val, up_val, sig, gate_val * sig


def down_kernel(n, rows, factors, at_ref, *refs):
    pairs, refs = refs[:n], refs[n:]
    grad_ref, keep_ref = refs[:2]
    buf, outs = refs[-1], refs[:-1]
    gdown_ref = outs[-3] if factors else outs[-1]
    if n == 1:
        hidden = pairs[0][...]
    else:
        gate = in_order(at_ref, buf, pairs, rows, 0)
        up = in_order(at_ref, buf, pairs, rows, 1)
        gate_val, up_val, sig, silu = gate_parts(gate, up)
        if factors:
            outs[-2][...] = up_val * sig * (1.0 + gate_val * (1.0 - sig))
            outs[-1][...] = silu
        hidden = (silu * up_val).astype(BF16)
    out = lax.dot_general(
        hidden, grad_ref[...], (((0,), (0,)), ((), ())), preferred_element_type=F32
    )
    gdown_ref[...] = masked(out, keep_ref[0]).astype(BF16)


def down_grad(where, pairs, grad_all, keep_down, held, at, f, n_row, ft, factors=False):
    T, D = grad_all.shape
    F = keep_down.shape[0] * ft
    rows, n = pairs[0].shape[0], len(pairs)
    first = held is None
    args = [where, *pairs, grad_all, keep_down]
    here = at // ft
    return pl.pallas_call(
        functools.partial(down_kernel, n, rows // 2, factors),
        out_shape=[jax.ShapeDtypeStruct((F, D), BF16)]
        + ([jax.ShapeDtypeStruct((T, f), F32)] * 2 if factors else []),
        grid_spec=pltpu.PrefetchScalarGridSpec(
            num_scalar_prefetch=1,
            grid=(f // ft,),
            in_specs=[pl.BlockSpec((rows, ft), lambda j, *_: (0, j))] * n
            + [whole((T, D)), pl.BlockSpec((1, ft // TILE, D), lambda j, *_: (j + here, 0, 0))]
            + ([] if first else [pl.BlockSpec(memory_space=pl.ANY)]),
            out_specs=[pl.BlockSpec((ft, D), lambda j, *_: (j + here, 0))]
            + ([pl.BlockSpec((T, ft), lambda j, *_: (0, j))] * 2 if factors else []),
            scratch_shapes=[pltpu.VMEM(((n_row + 1) * rows // 2, ft), BF16)],
        ),
        input_output_aliases={} if first else {len(args): 0},
        compiler_params=params(),
        cost_estimate=pl.CostEstimate(
            flops=2 * T * D * f, bytes_accessed=2 * D * f + 14 * T * f, transcendentals=T * f
        ),
        name="grad_down",
    )(*args, *([] if first else [held]))


def input_kernel(n, rows, n_pair, first, last, at_ref, *refs):
    pieces, refs = refs[:n], refs[n:]
    pairs, rest = refs[:n_pair], refs[n_pair:]
    wg_ref, wu_ref, kg_ref, ku_ref = rest[:4]
    rest = rest[4:]
    if not first:
        sum_ref, rest = rest[0], rest[1:]
    gx_ref, dg_ref, du_ref = rest[:3]
    buf, dg_all, du_all = rest[-3:]
    c = pl.program_id(1)

    @pl.when(pl.program_id(0) == 0)
    def _():
        d_hidden = in_order(at_ref, buf, pieces, rows).astype(F32)
        if n_pair == 2:
            d_gate = (d_hidden * pairs[0][...]).astype(BF16)
            d_up = (d_hidden * pairs[1][...]).astype(BF16)
        else:
            gate = in_order(at_ref, buf, pairs, rows, 0)
            up = in_order(at_ref, buf, pairs, rows, 1)
            gate_val, up_val, sig, silu = gate_parts(gate, up)
            d_gate = (d_hidden * up_val * sig * (1.0 + gate_val * (1.0 - sig))).astype(BF16)
            d_up = (d_hidden * silu).astype(BF16)
            if last:
                rest[4][...] = (silu * up_val).astype(BF16)
        dg_ref[...] = d_gate
        du_ref[...] = d_up
        dg_all[c] = d_gate
        du_all[c] = d_up

    dims = (((1,), (1,)), ((), ()))
    wg = masked(wg_ref[...], kg_ref[...].astype(BF16))
    wu = masked(wu_ref[...], ku_ref[...].astype(BF16))
    out = lax.dot_general(dg_all[c], wg, dims, preferred_element_type=F32)
    out = out + lax.dot_general(du_all[c], wu, dims, preferred_element_type=F32)

    @pl.when(c == 0)
    def _():
        gx_ref[...] = out if first else sum_ref[...] + out

    @pl.when(c > 0)
    def _():
        gx_ref[...] += out

    if last:

        @pl.when(c == pl.num_programs(1) - 1)
        def _():
            send_ref = rest[3]
            per = last
            for p in range(send_ref.shape[0] // per):
                start = pl.multiple_of((2 * p + 1 - at_ref[n]) * per, 8)
                send_ref[p * per : (p + 1) * per, :] = gx_ref[pl.ds(start, per), :]


def input_grad(where, pieces, pairs, w_gate, w_up, keep_gate, keep_up, total, span, last, n_row, ft, dt):
    rows, n = pieces[0].shape[0], len(pieces)
    T = rows * n_row
    D = w_gate.shape[0]
    start, width = span
    here, chunks = start // ft, width // ft
    first = total is None

    def once(d, c):
        return jnp.where(d == 0, c, chunks - 1)

    piece = pl.BlockSpec((rows, ft), lambda d, c, *_: (0, once(d, c)))
    pair = pl.BlockSpec((pairs[0].shape[0], ft), lambda d, c, *_: (0, once(d, c)))
    tall = pl.BlockSpec((T, ft), lambda d, c, *_: (0, once(d, c)))
    weight = pl.BlockSpec((dt, ft), lambda d, c, *_: (d, c + here))
    keep = pl.BlockSpec((dt // TILE, ft), lambda d, c, *_: (d, c + here))
    gx = pl.BlockSpec((T, dt), lambda d, c, *_: (0, d))
    args = [where, *pieces, *pairs, w_gate, w_up, keep_gate, keep_up]
    return pl.pallas_call(
        functools.partial(input_kernel, n, rows, len(pairs), first, last),
        out_shape=[
            jax.ShapeDtypeStruct((T, D), F32),
            jax.ShapeDtypeStruct((T, width), BF16),
            jax.ShapeDtypeStruct((T, width), BF16),
        ]
        + (
            [jax.ShapeDtypeStruct((T // 2, D), F32), jax.ShapeDtypeStruct((T, width), BF16)]
            if last
            else []
        ),
        grid_spec=pltpu.PrefetchScalarGridSpec(
            num_scalar_prefetch=1,
            grid=(D // dt, chunks),
            in_specs=[piece] * n
            + [pair] * len(pairs)
            + [weight, weight, keep, keep]
            + ([] if first else [gx]),
            out_specs=[gx, tall, tall]
            + ([pl.BlockSpec((T // 2, dt), lambda d, c, *_: (0, d)), tall] if last else []),
            scratch_shapes=[
                pltpu.VMEM(((n_row + 1) * rows, ft), BF16),
                pltpu.VMEM((chunks, T, ft), BF16),
                pltpu.VMEM((chunks, T, ft), BF16),
            ],
        ),
        input_output_aliases={} if first else {len(args): 0},
        compiler_params=params(2),
        cost_estimate=pl.CostEstimate(
            flops=4 * T * D * width, bytes_accessed=4 * D * width + 8 * T * D, transcendentals=T * width
        ),
        name="grad_x_part",
    )(*args, *([] if first else [total]))


def weight_kernel(tok_ref, dg_ref, du_ref, kg_ref, ku_ref, *refs):
    gg_ref, gu_ref = refs[-2:]
    tok = tok_ref[...]
    dims = (((0,), (0,)), ((), ()))
    gg = lax.dot_general(tok, dg_ref[...], dims, preferred_element_type=F32)
    gg_ref[...] = masked(gg, kg_ref[...]).astype(BF16)
    gu = lax.dot_general(tok, du_ref[...], dims, preferred_element_type=F32)
    gu_ref[...] = masked(gu, ku_ref[...]).astype(BF16)


def weight_grads(tok_all, d_gate, d_up, keep_gate, keep_up, held, span, part, ft):
    T, D = tok_all.shape
    F = keep_gate.shape[1]
    at, width = part[0] // ft, part[1]
    here = span[0] // ft + at
    keep = pl.BlockSpec((D // TILE, ft), lambda c: (0, c + here))
    out = pl.BlockSpec((D, ft), lambda c: (0, c + here))
    tall = pl.BlockSpec((T, ft), lambda c: (0, c + at))
    return pl.pallas_call(
        weight_kernel,
        out_shape=(jax.ShapeDtypeStruct((D, F), BF16),) * 2,
        grid=(width // ft,),
        in_specs=[whole((T, D)), tall, tall, keep, keep]
        + ([] if held is None else [pl.BlockSpec(memory_space=pl.ANY)] * 2),
        out_specs=[out, out],
        input_output_aliases={} if held is None else {5: 0, 6: 1},
        compiler_params=params(),
        cost_estimate=pl.CostEstimate(
            flops=4 * T * D * width, bytes_accessed=4 * D * width + 2 * T * D, transcendentals=0
        ),
        name="grad_gate_up",
    )(tok_all, d_gate, d_up, keep_gate, keep_up, *([] if held is None else held))


class Queue:
    def __init__(self, perm):
        self.perm, self.flying = perm, [(), ()]

    def hold(self, *deps):
        self.flying[0] = (*self.flying[0], *deps)

    def issue(self, x):
        wait = self.flying.pop(0)
        if wait:
            x, *_ = lax.optimization_barrier((x, *wait))
        x = lax.ppermute(x, "row", self.perm)
        self.flying.append((x,))
        return x


class Four:
    def __init__(self, me):
        self.me = me
        self.outer = Queue([(0, 1), (1, 0), (2, 3), (3, 2)])
        self.inner = Queue([(1, 2), (2, 1)])
        self.mid = (me == 1) | (me == 2)
        self.side = me // 2
        near, far = jnp.where(self.side == 0, 2, 1), jnp.where(self.side == 0, 3, 0)
        self.where = jnp.stack(
            [
                me,
                me ^ 1,
                jnp.where(self.mid, near, 4),
                jnp.where(self.mid, far, 4),
                jnp.where(self.mid, 4, near),
                jnp.where(self.mid, 4, far),
            ]
        ).astype(jnp.int32)


class Gather:
    def __init__(self, four, piece):
        self.four, self.own = four, piece

    def swap(self):
        self.next = self.four.outer.issue(self.own)

    def cross(self):
        self.near = self.four.inner.issue(self.own)

    def cross_next(self):
        self.far = self.four.inner.issue(self.next)

    def spread(self, outwards=None):
        send = self.near if outwards is None else jnp.where(self.four.mid, self.near, outwards)
        self.near_out = self.four.outer.issue(send)

    def spread_next(self):
        self.far_out = self.four.outer.issue(self.far)

    def pieces(self):
        return [self.own, self.next, self.near, self.far, self.near_out, self.far_out]


class Reduce:
    def __init__(self, four, part):
        self.four, self.part = four, part
        self.rows = part.shape[0] // 4

    def block(self, b, count=1):
        return lax.dynamic_slice_in_dim(self.part, b * self.rows, count * self.rows, 0)

    def others(self):
        return self.block(2 - 2 * self.four.side, 2)

    def cross(self, from_end):
        send = (self.others() + from_end.astype(F32)).astype(BF16)
        self.crossed = self.four.inner.issue(send)

    def crossed_block(self, b):
        got = lax.dynamic_slice_in_dim(self.crossed, (b % 2) * self.rows, self.rows, 0)
        return jnp.where(self.four.mid, got.astype(F32), 0.0)

    def swap(self):
        other = self.four.me ^ 1
        self.swapped = self.four.outer.issue(
            (self.block(other) + self.crossed_block(other)).astype(BF16)
        )

    def result(self):
        me = self.four.me
        return (self.block(me) + self.crossed_block(me) + self.swapped.astype(F32)).astype(BF16)


def ring_gather(piece, n):
    ring = [(i, (i + 1) % n) for i in range(n)]
    pieces = [piece]
    for _ in range(1, n):
        pieces.append(lax.ppermute(pieces[-1], "row", ring))
    return pieces


def ring_reduce(part, n, me):
    ring = [(i, (i + 1) % n) for i in range(n)]
    rows = part.shape[0] // n
    total = None
    for s in range(n):
        block = lax.dynamic_slice_in_dim(part, (me + n - 1 - s) % n * rows, rows, 0)
        total = block if total is None else block + total.astype(F32)
        total = total.astype(BF16)
        if s < n - 1:
            total = lax.ppermute(total, "row", ring)
    return total


def pairs_gather(piece, n, in_turn=False):
    got = [piece]
    for k in range(1, n // 2):
        send = lax.optimization_barrier((piece, got[-1]))[0] if in_turn else piece
        got.append(lax.ppermute(send, "col", [(i, i ^ (2 * k)) for i in range(n)]))
    return jnp.stack(got)


def pair_gather(mine, n, me):
    half, rows, width = mine.shape
    core, pair = me % 2, me // 2
    other = lax.ppermute(mine, "col", [(i, i ^ 1) for i in range(n)])
    even, odd = jnp.where(core == 0, mine, other), jnp.where(core == 0, other, mine)
    both = jnp.stack([even, odd], axis=1)
    ordered = [lax.dynamic_index_in_dim(both, pair ^ k, 0, keepdims=False) for k in range(half)]
    return jnp.stack(ordered).reshape(n * rows, width)


def pair_sums(part, send, n, me):
    rows = part.shape[0] // n
    core = me % 2
    blocks = part.reshape(n // 2, 2, rows, part.shape[1])
    send = send.reshape(n // 2, rows, part.shape[1])
    keep = lax.dynamic_index_in_dim(blocks, core, 1, keepdims=False)
    return keep + lax.ppermute(send, "col", [(i, i ^ 1) for i in range(n)])


def pair_reduce(summed, n, me):
    half = n // 2
    pair = me // 2
    total = lax.dynamic_index_in_dim(summed, pair, 0, keepdims=False)
    low = summed.astype(BF16)
    got = [
        lax.ppermute(
            lax.dynamic_index_in_dim(low, pair ^ k, 0, keepdims=False),
            "col",
            [(i, i ^ (2 * k)) for i in range(n)],
        )
        for k in range(1, half)
    ]
    for g in got:
        total = total + g.astype(F32)
    return total


def lanes(mask):
    return jnp.repeat(mask.astype(F32), TILE, axis=1)


def per_device(
    n_row,
    n_col,
    tokens,
    out_grad,
    gate_pre,
    up_pre,
    w_gate,
    w_up,
    w_down,
    mask_gate,
    mask_up,
    mask_down,
):
    row, col = lax.axis_index("row"), lax.axis_index("col")
    F, D = w_down.shape
    ft = 512 if F % 512 == 0 else 256
    dt = min(2048, D)
    keep_gate, keep_up, keep_down = lanes(mask_gate), lanes(mask_up), lanes(mask_down)
    keep_down = keep_down.reshape(F // ft, ft // TILE, D)

    n_tiles = F // ft
    cut = (n_tiles + 1) // 2 * ft
    spans = ((0, cut), (cut, F - cut))
    own = [
        jnp.concatenate([gate_pre[:, a : a + f], up_pre[:, a : a + f]], axis=0) for a, f in spans
    ]

    def use(which, pieces, pairs, total):
        last = grad_all.shape[0] // n_col if which else 0
        return input_grad(
            where, pieces, pairs, w_gate, w_up, keep_gate, keep_up, total, spans[which], last, n_row, ft, dt
        )

    def weights(which, d_gate, d_up, held, part=None):
        span = spans[which]
        part = part or (0, span[1])
        return weight_grads(tok_all, d_gate, d_up, keep_gate, keep_up, held, span, part, ft)

    def down(which, pairs, grad_down, factors=False):
        start, width = spans[which]
        return down_grad(
            where, pairs, grad_all, keep_down, grad_down, start, width, n_row, ft, factors
        )

    if n_row != 4:
        where = jnp.stack([(row - s) % n_row for s in range(n_row)] + [col % 2]).astype(jnp.int32)
        grad_all = pair_gather(pairs_gather(out_grad, n_col), n_col, col)
        tok_all = pair_gather(pairs_gather(tokens, n_col), n_col, col)
        total = held = grad_down = None
        for which, span in enumerate(spans):
            part = dhidden_part(grad_all, w_down, keep_down, span, ft)
            pairs = ring_gather(own[which], n_row)
            pieces = ring_gather(ring_reduce(part, n_row, row), n_row)
            total, d_gate, d_up, *send = use(which, pieces, pairs, total)
            held = weights(which, d_gate, d_up, held)
            (grad_down,) = down(which, pairs, grad_down)
        grad_x = pair_reduce(pair_sums(total, send[0], n_col, col), n_col, col).astype(BF16)
        return (grad_x, held[0], held[1], grad_down)

    def after(x, *deps):
        return lax.optimization_barrier((x, *deps))[0]

    four = Four(row)
    where = jnp.append(four.where, (col % 2).astype(jnp.int32))
    outer, inner = four.outer, four.inner
    a, b = Gather(four, own[0]), Gather(four, own[1])
    a.swap()
    a.cross()
    mine = pairs_gather(out_grad, n_col)
    grad_all = pair_gather(after(mine, a.next, a.near, keep_down, keep_gate, keep_up), n_col, col)
    b.swap()
    b.cross()
    low = dhidden_part(grad_all, w_down, keep_down, spans[0], ft)
    sum_a = Reduce(four, low)
    outwards = sum_a.others().astype(BF16)
    outer.hold(b.next, b.near)
    a.spread(outwards)
    sum_b = Reduce(four, dhidden_part(grad_all, w_down, keep_down, spans[1], ft))
    inner.hold(outwards)
    a.cross_next()
    tok_mine = pairs_gather(after(tokens, a.far), n_col, True)
    b_outwards = sum_b.others().astype(BF16)
    b.spread(b_outwards)
    inner.hold(b_outwards)
    sum_a.cross(a.near_out)
    outer.hold(b.near_out)
    a.spread_next()
    b.cross_next()
    sum_b.cross(b.near_out)
    outer.hold(a.far_out, b.far)
    sum_a.swap()
    tok_all = pair_gather(tok_mine, n_col, col)
    h_a = Gather(four, sum_a.result())
    h_a.cross()
    h_a.swap()
    sum_b.swap()
    grad_down, *factors = down(0, a.pieces(), None, True)
    inner.hold(grad_down, h_a.near)
    h_a.spread()
    h_a.cross_next()
    h_b = Gather(four, sum_b.result())
    h_b.cross()
    outer.hold(h_a.near_out)
    h_a.spread_next()
    outer.hold(tok_all)
    h_b.swap()
    b.spread_next()
    total, d_gate, d_up = use(0, h_a.pieces(), factors, None)
    inner.hold(total)
    h_b.cross_next()
    outer.hold(total)
    h_b.spread()
    half = cut // ft // 2 * ft
    held = weights(0, d_gate, d_up, None, (0, half))
    outer.hold(held[0])
    h_b.spread_next()
    held = weights(0, d_gate, d_up, held, (half, cut - half))
    total = after(total, held[0])
    total, d_gate, d_up, send, hidden = use(1, h_b.pieces(), b.pieces(), total)
    summed = pair_sums(total, send, n_col, col)
    (grad_down,) = down(1, [hidden], grad_down)
    grad_x = pair_reduce(summed, n_col, col).astype(BF16)
    held = weights(1, after(d_gate, summed), d_up, held)
    return (grad_x, held[0], held[1], grad_down)


def solution(mesh):
    return jax.shard_map(
        functools.partial(per_device, mesh.shape["row"], mesh.shape["col"]),
        mesh=mesh,
        in_specs=(
            P("col", "row"),
            P("col", "row"),
            P("row", "col"),
            P("row", "col"),
            P("row", "col"),
            P("row", "col"),
            P("col", "row"),
            P("row", "col"),
            P("row", "col"),
            P("col", "row"),
        ),
        out_specs=(P("col", "row"), P("row", "col"), P("row", "col"), P("col", "row")),
        check_vma=False,
    )
```
